512 devices in a mesh: frame: 128 (over y, z_lo, x), space: 4 (over z_hi, core).
Axes of the slice: x: 4, y: 4, z: 16 (z_hi: 2, z_lo: 8; z = z_hi * 8 + z_lo), core: 2. Of those that a mesh axis runs over, the one named last changes fastest.
Arguments:
- query_vectors: bfloat16 [512, 12, 12, 1024], P('frame', 'space'), may hold values from -6 to 6
- key_vectors: bfloat16 [512, 12, 12, 1024], P('frame', 'space'), may hold values from -6 to 6
- value_vectors: bfloat16 [512, 12, 12, 1024], P('frame', 'space'), may hold values from -6 to 6
- out_cotangent: bfloat16 [512, 12, 12, 1024], P('frame', 'space'), may hold values from -6 to 6
- partner_mask: int32 [512, 4], replicated, may hold values 0 or 1
Outputs:
- attended: bfloat16 [512, 12, 12, 1024], P('frame', 'space')
- query_grad: bfloat16 [512, 12, 12, 1024], P('frame', 'space')
- key_grad: bfloat16 [512, 12, 12, 1024], P('frame', 'space')
- value_grad: bfloat16 [512, 12, 12, 1024], P('frame', 'space')
The draws below stay inside these ranges and needn't reach their ends.
All inputs are finite; a program needn't handle non-finite values.
Results may differ from the reference program's by a relative error of at most 0.011.
Values may be sent and summed in bfloat16 or wider, within the bound.
A program may use at most 128 MiB of HBM per device.

```python
import jax
import jax.numpy as jnp
from jax import lax

HEADS = 16
HEAD_DIM = 64
ROWS = 12
COLS = 12
FR_DEV = 4
D = 1024
FRAMES = 512
PARTNERS = 4
N_FRAME = 128


def base_field(key):
    shape = (FRAMES, ROWS, COLS, HEADS * HEAD_DIM)
    return jnp.clip(jax.random.normal(key, shape, jnp.float32), -6.0, 6.0)


def draw_query_vectors(key, part):
    field = base_field(jax.random.fold_in(key, 1))
    return field.astype(jnp.bfloat16)


def draw_key_vectors(key, part):
    field = base_field(jax.random.fold_in(key, 2))
    return field.astype(jnp.bfloat16)


def set_ends(entries, own_key, low, top_value):
    longest = entries.shape.index(max(entries.shape))
    spots = []
    for shift in (0, 1):
        where = [jax.random.randint(jax.random.fold_in(own_key, axis), (), 0, length) for axis, length in enumerate(entries.shape)]
        where[longest] = (where[longest] + shift) % entries.shape[longest]
        spots.append(tuple(where))
    return entries.at[spots[0]].set(low).at[spots[1]].set(top_value)


def block_scale(rng, shape, pieces, low, largest):
    gain = 1.0
    for axis_at, shards_of in pieces:
        draws = jax.random.uniform(jax.random.fold_in(jax.random.fold_in(rng, 6), axis_at), (shards_of,), jnp.float32, low / len(pieces), largest / len(pieces))
        gain = gain * jnp.repeat(jnp.exp(draws), shape[axis_at] // shards_of).reshape((-1,) + (1,) * (len(shape) - 1 - axis_at))
    return gain


def centred(rng, shape, deviation, most, shards=(), kind=jnp.bfloat16):
    values = deviation * jax.random.normal(rng, shape, jnp.float32)
    if shards:
        values = values * block_scale(rng, shape, shards, -0.22, 0.18)
    return jnp.clip(values, -most, most).astype(kind)


def setup_inputs(seed: int = 0) -> dict:
    splits = jax.random.split(jax.random.key(seed), 6)
    return {
        "query_vectors": draw_query_vectors(jax.random.fold_in(splits[5], 71), 0),
        "key_vectors": draw_key_vectors(jax.random.fold_in(splits[5], 71), 0),
        "value_vectors": centred(splits[2], (FRAMES, ROWS, COLS, D), 1.0, 6.0, ((0, 128), (1, 4))),
        "out_cotangent": centred(splits[3], (FRAMES, ROWS, COLS, D), 1.0, 6.0, ((0, 128), (1, 4))),
        "partner_mask": set_ends((jax.random.randint(splits[4], (FRAMES, PARTNERS), 0, 4) < 3).astype(jnp.int32), jax.random.fold_in(splits[4], 1), 0, 1),
    }


SCALE = 0.125
NEG = -1.0e30


def partners(group):
    return jnp.stack([group] + [jnp.bitwise_xor(group, 1 << which_bit) for which_bit in range(PARTNERS)]).astype(jnp.int32)


def windows(blockwise):
    padded = jnp.pad(blockwise, ((0, 0), (0, 0), (1, 1), (0, 0), (0, 0)))
    stacked = jnp.stack([padded[:, :, start:start + 3] for start in range(ROWS)])
    return stacked.reshape(ROWS, -1, blockwise.shape[-1])


def reference(query_vectors, key_vectors, value_vectors, out_cotangent, partner_mask):
    width = HEADS * HEAD_DIM
    blocks = PARTNERS + 1
    queries5 = query_vectors.reshape(N_FRAME, FR_DEV, ROWS, COLS, width)
    keys5 = key_vectors.reshape(N_FRAME, FR_DEV, ROWS, COLS, width)
    values5 = value_vectors.reshape(N_FRAME, FR_DEV, ROWS, COLS, width)
    grads5 = out_cotangent.reshape(N_FRAME, FR_DEV, ROWS, COLS, width)
    masks = partner_mask.reshape(N_FRAME, FR_DEV, PARTNERS) == 1
    near_rows = jnp.arange(ROWS)[:, None] + jnp.arange(3)[None, :] - 1
    row_valid = (near_rows >= 0) & (near_rows < ROWS)

    def own_rows(array):
        return array.transpose(1, 0, 2, 3).reshape(ROWS, -1, HEADS, HEAD_DIM).astype(jnp.float32)

    def forward_block(group):
        members = partners(group)
        key_win = windows(keys5[members]).reshape(ROWS, -1, HEADS, HEAD_DIM).astype(jnp.float32)
        value_win = windows(values5[members]).reshape(ROWS, -1, HEADS, HEAD_DIM).astype(jnp.float32)
        query_now = own_rows(queries5[group])
        grad_now = own_rows(grads5[group])
        block_ok = jnp.concatenate([jnp.ones((FR_DEV, 1), bool), masks[group]], axis=1)
        allowed = block_ok[None, :, None, :, None, None, None] & row_valid[:, None, None, None, None, :, None]
        allowed = jnp.broadcast_to(allowed, (ROWS, FR_DEV, COLS, blocks, FR_DEV, 3, COLS)).reshape(ROWS, FR_DEV * COLS, -1)
        scores = jnp.einsum("rqhe,rkhe->rhqk", query_now, key_win) * SCALE
        masked = jnp.where(allowed[:, None], scores, NEG)
        top = jnp.max(masked, axis=3, keepdims=True)
        total = jnp.sum(jnp.exp(masked - top), axis=3, keepdims=True)
        log_total = top + jnp.log(total)
        probs = jnp.exp(masked - log_total)
        weights = lax.optimization_barrier(probs.astype(jnp.bfloat16))
        attended = jnp.einsum("rhqk,rkhe->rqhe", weights.astype(jnp.float32), value_win).astype(jnp.bfloat16)
        attended = lax.optimization_barrier(attended)
        delta = jnp.sum(grad_now * attended.astype(jnp.float32), axis=3)
        grad_probs = jnp.einsum("rqhe,rkhe->rhqk", grad_now, value_win)
        grad_scores = (probs * (grad_probs - delta.transpose(0, 2, 1)[..., None])).astype(jnp.bfloat16)
        grad_scores = lax.optimization_barrier(grad_scores)
        query_grad = (jnp.einsum("rhqk,rkhe->rqhe", grad_scores.astype(jnp.float32), key_win) * SCALE).astype(jnp.bfloat16)
        lse = log_total[..., 0].transpose(0, 2, 1).reshape(ROWS, FR_DEV, COLS, HEADS).transpose(1, 0, 2, 3)
        delta_out = delta.reshape(ROWS, FR_DEV, COLS, HEADS).transpose(1, 0, 2, 3)
        attended = attended.reshape(ROWS, FR_DEV, COLS, width).transpose(1, 0, 2, 3)
        query_grad = query_grad.reshape(ROWS, FR_DEV, COLS, width).transpose(1, 0, 2, 3)
        return attended, query_grad, lse, delta_out

    groups = jnp.arange(N_FRAME, dtype=jnp.int32)
    attended, query_grad, lse_all, delta_all = lax.map(forward_block, groups)

    def backward_block(group):
        members = partners(group)
        query_win = windows(queries5[members]).reshape(ROWS, -1, HEADS, HEAD_DIM).astype(jnp.float32)
        grad_win = windows(grads5[members]).reshape(ROWS, -1, HEADS, HEAD_DIM).astype(jnp.float32)
        lse_win = windows(lse_all[members]).reshape(ROWS, -1, HEADS)
        delta_win = windows(delta_all[members]).reshape(ROWS, -1, HEADS)
        key_now = own_rows(keys5[group])
        value_now = own_rows(values5[group])
        partner_ok = jnp.stack([jnp.ones((FR_DEV,), bool)] + [masks[members[1 + which_bit]][:, which_bit] for which_bit in range(PARTNERS)])
        allowed = partner_ok[None, :, :, None, None, None, None] & row_valid[:, None, None, :, None, None, None]
        allowed = jnp.broadcast_to(allowed, (ROWS, blocks, FR_DEV, 3, COLS, FR_DEV, COLS)).reshape(ROWS, -1, FR_DEV * COLS)
        scores = jnp.einsum("rqhe,rkhe->rhqk", query_win, key_now) * SCALE
        probs = jnp.exp(jnp.where(allowed[:, None], scores - lse_win.transpose(0, 2, 1)[..., None], NEG))
        weights = lax.optimization_barrier(probs.astype(jnp.bfloat16))
        value_grad = jnp.einsum("rhqk,rqhe->rkhe", weights.astype(jnp.float32), grad_win).astype(jnp.bfloat16)
        grad_probs = jnp.einsum("rqhe,rkhe->rhqk", grad_win, value_now)
        grad_scores = (probs * (grad_probs - delta_win.transpose(0, 2, 1)[..., None])).astype(jnp.bfloat16)
        grad_scores = lax.optimization_barrier(grad_scores)
        key_grad = (jnp.einsum("rhqk,rqhe->rkhe", grad_scores.astype(jnp.float32), query_win) * SCALE).astype(jnp.bfloat16)
        key_grad = key_grad.reshape(ROWS, FR_DEV, COLS, width).transpose(1, 0, 2, 3)
        value_grad = value_grad.reshape(ROWS, FR_DEV, COLS, width).transpose(1, 0, 2, 3)
        return key_grad, value_grad

    key_grad, value_grad = lax.map(backward_block, groups)
    full = (FRAMES, ROWS, COLS, width)
    return (attended.reshape(full), query_grad.reshape(full), key_grad.reshape(full), value_grad.reshape(full))
```

```python
import functools

import jax
import jax.numpy as jnp
from jax import lax
from jax.experimental import pallas as pl
from jax.experimental.pallas import tpu as pltpu
from jax.sharding import PartitionSpec as P

HEAD_DIM = 64
SCALE = 0.125
NEG = -1e30
WIDE = 256
HEADS = WIDE // HEAD_DIM
STATS = 3 * HEADS
F32 = jnp.float32
BF16 = jnp.bfloat16


def dot_nt(a, b):
    return lax.dot_general(a, b, (((1,), (1,)), ((), ())), preferred_element_type=F32)


def dot_nn(a, b):
    return lax.dot_general(a, b, (((1,), (0,)), ((), ())), preferred_element_type=F32)


def dot_tn(a, b):
    return lax.dot_general(a, b, (((0,), (0,)), ((), ())), preferred_element_type=F32)


def kernel(
    dims, kv_ref, qg_ref, bias_ref, o_ref, dq_ref, dk_ref, dv_ref,
    kvx, halo, qm, gm, pm, ot, stat, stat_in, wm, dm, oq, rim_out, rim_in, dkv, dkv_out, dkv_in,
    kv_ss, kv_rs, halo_ss, halo_rs, stat_ss, stat_rs, rim_ss, rim_rs, dkv_ss, dkv_rs,
):
    chunks, rows, tok, bits, space, keys = dims
    ext = rows + 2
    frame_at = lax.axis_index("frame")
    space_at = lax.axis_index("space")
    partner = []
    for b in range(bits):
        step = 1 << b
        partner.append(frame_at + step * (1 - 2 * ((frame_at // step) % 2)))
    has = (space_at > 0, space_at < space - 1)
    near = (space_at - 1, space_at + 1)

    def remote(src, dst, send, recv, frame, band):
        return pltpu.make_async_remote_copy(
            src_ref=src, dst_ref=dst, send_sem=send, recv_sem=recv,
            device_id=(frame, band), device_id_type=pl.DeviceIdType.MESH,
        )

    def kv_copy(c, b):
        return remote(
            kv_ref.at[c], kvx.at[c, :, :, pl.ds(tok * (b + 1), tok)],
            kv_ss.at[c, b], kv_rs.at[c, b], partner[b], space_at,
        )

    def dkv_copy(c, b):
        return remote(
            dkv_out.at[c, b], dkv_in.at[c, b], dkv_ss.at[c, b], dkv_rs.at[c, b], partner[b], space_at
        )

    def halo_copy(c, s):
        return remote(
            qg_ref.at[c, :, 0 if s == 0 else rows - 1], halo.at[c, 1 - s],
            halo_ss.at[c, s], halo_rs.at[c, 1 - s], frame_at, near[s],
        )

    def stat_copy(c, s):
        return remote(
            stat.at[c, 2 * s], stat_in.at[c, 1 - s],
            stat_ss.at[c, s], stat_rs.at[c, 1 - s], frame_at, near[s],
        )

    def rim_copy(c, s):
        return remote(
            rim_out.at[c, s], rim_in.at[c, 1 - s],
            rim_ss.at[c, s], rim_rs.at[c, 1 - s], frame_at, near[s],
        )

    def start_sides(copy, c):
        for s in range(2):
            @pl.when(has[s])
            def _():
                copy(c, s).start()

    def wait_sides(copy, c):
        for s in range(2):
            @pl.when(has[s])
            def _():
                copy(c, 1 - s).wait_recv()

    def wait_sent_sides(copy, c):
        for s in range(2):
            @pl.when(has[s])
            def _():
                copy(c, s).wait_send()

    barrier = pltpu.get_barrier_semaphore()
    for b in range(bits):
        pl.semaphore_signal(
            barrier, inc=1, device_id=(partner[b], space_at), device_id_type=pl.DeviceIdType.MESH
        )
    for s in range(2):
        @pl.when(has[s])
        def _():
            pl.semaphore_signal(
                barrier, inc=1, device_id=(frame_at, near[s]), device_id_type=pl.DeviceIdType.MESH
            )
    pl.semaphore_wait(barrier, bits + has[0].astype(jnp.int32) + has[1].astype(jnp.int32))

    def send_first(c, carry):
        for b in reversed(range(bits)):
            kv_copy(c, b).start()
        start_sides(halo_copy, c)
        return carry

    lax.fori_loop(0, chunks, send_first, 0)

    lane = lax.broadcasted_iota(jnp.int32, (tok, 128), 1)
    low = lane < HEAD_DIM

    for s in range(2):
        @pl.when(jnp.logical_not(has[s]))
        def _():
            halo[:, s] = jnp.zeros(halo.shape[:1] + halo.shape[2:], BF16)
            rim_in[:, s] = jnp.zeros(rim_in.shape[:1] + rim_in.shape[2:], BF16)
            top_lane = lane - (lane // STATS) * STATS < HEADS
            stat_in[:, s] = jnp.broadcast_to(
                jnp.where(top_lane, NEG, 0.0).astype(F32)[None], (chunks, tok, 128)
            )

    def stacked(block):
        wide = block.astype(F32)
        zero = jnp.zeros((tok, 128), F32)
        out = []
        for h in range(HEADS):
            half = wide[:, 128 * (h // 2) : 128 * (h // 2) + 128]
            kept = jnp.where(low if h % 2 == 0 else jnp.logical_not(low), half, zero)
            out.append(jnp.concatenate([kept, zero] if h < 2 else [zero, kept], axis=1))
        return jnp.concatenate(out, axis=0).astype(BF16)

    def picked(full):
        return jnp.concatenate(
            [
                jnp.where(low, full[:tok, :128], full[tok : 2 * tok, :128]),
                jnp.where(low, full[2 * tok : 3 * tok, 128:], full[3 * tok :, 128:]),
            ],
            axis=1,
        )

    def forward(c):
        kvx[c, :, :, :tok, :] = kv_ref[c]
        spare = keys - tok * (bits + 1)
        if spare:
            kvx[c, :, :, keys - spare :, :] = jnp.zeros((2, rows, spare, WIDE), BF16)
        bias = jnp.concatenate([bias_ref[...]] * HEADS, axis=0)
        tiles = [jnp.zeros((tok, 128), F32) for _ in range(3)]
        for i in range(ext):
            if i == 0 or i == ext - 1:
                query, grad = halo[c, 0 if i == 0 else 1, 0], halo[c, 0 if i == 0 else 1, 1]
            else:
                query, grad = qg_ref[c, 0, i - 1], qg_ref[c, 1, i - 1]
            query = stacked(query)
            grad = stacked(grad)
            qm[c, i] = query
            gm[c, i] = grad
            near_rows = [r for r in range(rows) if 0 <= i - r <= 2]
            scores = [dot_nt(query, kvx[c, 0, r]) + bias for r in near_rows]
            top = jnp.max(functools.reduce(jnp.maximum, scores), axis=1, keepdims=True)
            probs = [jnp.exp(one - top) for one in scores]
            total = jnp.sum(functools.reduce(jnp.add, probs), axis=1, keepdims=True)
            full = None
            for r, prob in zip(near_rows, probs):
                prob = prob.astype(BF16)
                pm[c, r, i - r] = prob
                part = dot_nn(prob, kvx[c, 1, r])
                full = part if full is None else full + part
            ot[c, i] = picked(full)
            place = 0 if i < 2 else (1 if i < ext - 2 else 2)
            base = STATS * (1 if i in (1, ext - 1) else 0)
            for h in range(HEADS):
                span = slice(h * tok, (h + 1) * tok)
                half = slice(128 * (h // 2), 128 * (h // 2) + 128)
                delta = jnp.sum(
                    full[span, half] * grad[span, half].astype(F32), axis=1, keepdims=True
                )
                for kind, value in enumerate((top[span], total[span], delta)):
                    tiles[place] = jnp.where(lane == base + kind * HEADS + h, value, tiles[place])
        for place in range(3):
            stat[c, place] = tiles[place]

    def backward(c):
        alphas, deltas = [], []
        for place in range(3):
            mine = stat[c, place]
            top, total, delta = mine, pltpu.roll(mine, 128 - HEADS, 1), pltpu.roll(mine, 128 - 2 * HEADS, 1)
            if place == 1:
                alphas.append(1.0 / total)
                deltas.append(delta / total)
                continue
            theirs = stat_in[c, 0 if place == 0 else 1]
            top2, total2, delta2 = (
                theirs, pltpu.roll(theirs, 128 - HEADS, 1), pltpu.roll(theirs, 128 - 2 * HEADS, 1)
            )
            best = jnp.maximum(top, top2)
            part, part2 = jnp.exp(top - best), jnp.exp(top2 - best)
            inverse = 1.0 / (total * part + total2 * part2)
            alphas.append(part * inverse)
            deltas.append((delta * part + delta2 * part2) * inverse)
        for i in range(ext):
            place = 0 if i < 2 else (1 if i < ext - 2 else 2)
            base = STATS * (1 if i in (1, ext - 1) else 0)
            alpha_h = [alphas[place][:, base + h : base + h + 1] for h in range(HEADS)]
            alpha = jnp.concatenate(alpha_h, axis=0)
            delta = jnp.concatenate(
                [deltas[place][:, base + h : base + h + 1] for h in range(HEADS)], axis=0
            )
            full = None
            for r in range(rows):
                if not 0 <= i - r <= 2:
                    continue
                grad_prob = dot_nt(gm[c, i], kvx[c, 1, r])
                weight = pm[c, r, i - r].astype(F32) * alpha
                grad_score = (weight * (grad_prob - delta)).astype(BF16)
                wm[r, i - r] = weight.astype(BF16)
                dm[r, i - r] = grad_score
                part = dot_nn(grad_score, kvx[c, 0, r])
                full = part if full is None else full + part
            query_grad = picked(full) * SCALE
            spread = jnp.concatenate(
                [jnp.where(low, alpha_h[0], alpha_h[1]), jnp.where(low, alpha_h[2], alpha_h[3])], axis=1
            )
            attended = ot[c, i] * spread
            if i == 0 or i == ext - 1:
                s = 0 if i == 0 else 1
                rim_out[c, s, 0] = attended.astype(BF16)
                rim_out[c, s, 1] = query_grad.astype(BF16)
            else:
                oq[c, 0, i - 1] = attended
                oq[c, 1, i - 1] = query_grad
        for r in range(rows):
            grads = gm[c, r : r + 3].reshape(3 * HEADS * tok, WIDE)
            queries = qm[c, r : r + 3].reshape(3 * HEADS * tok, WIDE)
            key_grad = dot_tn(dm[r].reshape(3 * HEADS * tok, keys), queries)
            value_grad = dot_tn(wm[r].reshape(3 * HEADS * tok, keys), grads)
            for which, result in enumerate((key_grad, value_grad)):
                dkv[c, which, r] = result[:tok]
                for b in range(bits):
                    dkv_out[c, b, which, r] = result[tok * (b + 1) : tok * (b + 2)].astype(BF16)

    def step(t, carry):
        @pl.when(t < chunks)
        def _():
            for b in range(bits):
                kv_copy(t, b).wait_recv()
            wait_sides(halo_copy, t)
            forward(t)
            start_sides(stat_copy, t)

        @pl.when(t > 0)
        def _():
            wait_sides(stat_copy, t - 1)
            backward(t - 1)
            for b in reversed(range(bits)):
                dkv_copy(t - 1, b).start()
            start_sides(rim_copy, t - 1)

        return carry

    lax.fori_loop(0, chunks + 1, step, 0)

    def finish(c, carry):
        wait_sides(rim_copy, c)
        for r in range(rows):
            for which, out in enumerate((o_ref, dq_ref)):
                result = oq[c, which, r]
                if r == 0:
                    result = result + rim_in[c, 0, which].astype(F32)
                if r == rows - 1:
                    result = result + rim_in[c, 1, which].astype(F32)
                out[c, r] = result.astype(BF16)
        for b in range(bits):
            dkv_copy(c, b).wait_recv()
        for r in range(rows):
            for which, out in enumerate((dk_ref, dv_ref)):
                result = dkv[c, which, r]
                for b in range(bits):
                    result = result + dkv_in[c, b, which, r].astype(F32)
                out[c, r] = result.astype(BF16)
        return carry

    lax.fori_loop(0, chunks, finish, 0)

    def drain(c, carry):
        for b in range(bits):
            kv_copy(c, b).wait_send()
            dkv_copy(c, b).wait_send()
        wait_sent_sides(halo_copy, c)
        wait_sent_sides(stat_copy, c)
        wait_sent_sides(rim_copy, c)
        return carry

    lax.fori_loop(0, chunks, drain, 0)


def per_device(query_vectors, key_vectors, value_vectors, out_cotangent, partner_mask):
    frames, rows, cols, width = query_vectors.shape
    bits = min(4, lax.axis_size("frame").bit_length() - 1)
    space = lax.axis_size("space")
    chunks = width // WIDE
    tok = frames * cols
    keys = -(-tok * (bits + 1) // 128) * 128
    ext = rows + 2

    def lay(array):
        return array.reshape(frames, rows, cols, chunks, WIDE).transpose(3, 1, 0, 2, 4).reshape(
            chunks, rows, tok, WIDE
        )

    def back(array):
        return array.reshape(chunks, rows, frames, cols, WIDE).transpose(2, 1, 3, 0, 4).reshape(
            frames, rows, cols, width
        )

    kv = jnp.stack([lay(key_vectors), lay(value_vectors)], axis=1)
    qg = jnp.stack([lay(query_vectors * SCALE), lay(out_cotangent)], axis=1)
    own = lax.dynamic_slice_in_dim(partner_mask, lax.axis_index("frame") * frames, frames, 0)[:, :bits] == 1
    allowed = jnp.concatenate([jnp.ones((frames, 1), bool), own], axis=1)
    allowed = jnp.repeat(jnp.repeat(allowed, cols, axis=0), tok, axis=1)
    allowed = jnp.pad(allowed, ((0, 0), (0, keys - allowed.shape[1])))
    bias = jnp.where(allowed, 0.0, NEG).astype(F32)

    dims = (chunks, rows, tok, bits, space, keys)
    out = jax.ShapeDtypeStruct((chunks, rows, tok, WIDE), BF16)
    vmem = pl.BlockSpec(memory_space=pltpu.VMEM)
    stack = HEADS * tok
    dma = pltpu.SemaphoreType.DMA
    results = pl.pallas_call(
        functools.partial(kernel, dims),
        out_shape=(out,) * 4,
        in_specs=[vmem] * 3,
        out_specs=(vmem,) * 4,
        scratch_shapes=[
            pltpu.VMEM((chunks, 2, rows, keys, WIDE), BF16),
            pltpu.VMEM((chunks, 2, 2, tok, WIDE), BF16),
            pltpu.VMEM((chunks, ext, stack, WIDE), BF16),
            pltpu.VMEM((chunks, ext, stack, WIDE), BF16),
            pltpu.VMEM((chunks, rows, 3, stack, keys), BF16),
            pltpu.VMEM((chunks, ext, tok, WIDE), F32),
            pltpu.VMEM((chunks, 3, tok, 128), F32),
            pltpu.VMEM((chunks, 2, tok, 128), F32),
            pltpu.VMEM((rows, 3, stack, keys), BF16),
            pltpu.VMEM((rows, 3, stack, keys), BF16),
            pltpu.VMEM((chunks, 2, rows, tok, WIDE), F32),
            pltpu.VMEM((chunks, 2, 2, tok, WIDE), BF16),
            pltpu.VMEM((chunks, 2, 2, tok, WIDE), BF16),
            pltpu.VMEM((chunks, 2, rows, tok, WIDE), F32),
            pltpu.VMEM((chunks, bits, 2, rows, tok, WIDE), BF16),
            pltpu.VMEM((chunks, bits, 2, rows, tok, WIDE), BF16),
            dma((chunks, bits)), dma((chunks, bits)),
            dma((chunks, 2)), dma((chunks, 2)),
            dma((chunks, 2)), dma((chunks, 2)),
            dma((chunks, 2)), dma((chunks, 2)),
            dma((chunks, bits)), dma((chunks, bits)),
        ],
        compiler_params=pltpu.CompilerParams(
            collective_id=0, has_side_effects=True, vmem_limit_bytes=56 * 1024 * 1024
        ),
        name="butterfly",
    )(kv, qg, bias)
    return tuple(back(result) for result in results)


def solution(mesh):
    spread = P("frame", "space", None, None)
    return jax.shard_map(
        per_device,
        mesh=mesh,
        in_specs=(spread,) * 4 + (P(),),
        out_specs=(spread,) * 4,
        check_vma=False,
    )
```

```python
import functools

import jax
import jax.numpy as jnp
from jax import lax
from jax.experimental import pallas as pl
from jax.experimental.pallas import tpu as pltpu
from jax.sharding import PartitionSpec as P

HEAD_DIM = 64
SCALE = 0.125
NEG = -1e30
AHEAD = 2
WIDE = 256
HEADS = WIDE // HEAD_DIM
STATS = 4 * HEADS
F32 = jnp.float32
BF16 = jnp.bfloat16


def dot_nt(a, b):
    return lax.dot_general(a, b, (((1,), (1,)), ((), ())), preferred_element_type=F32)


def dot_nn(a, b):
    return lax.dot_general(a, b, (((1,), (0,)), ((), ())), preferred_element_type=F32)


def dot_tn(a, b):
    return lax.dot_general(a, b, (((0,), (0,)), ((), ())), preferred_element_type=F32)


def kernel(
    dims, q_hbm, k_hbm, v_hbm, g_hbm, mask_hbm, out_ref,
    k_ref, v_ref, q_ref, g_ref, mask_ref, kvx, qg, halo, bias_at, qm, gm, pm, ot, stat, stat_in, wm, dm, oq, rim_out, rim_in, dkv, dkv_out, dkv_in,
    kv_ss, kv_rs, halo_ss, halo_rs, stat_ss, stat_rs, rim_ss, rim_rs, dkv_ss, dkv_rs, load_sem,
):
    chunks, rows, tok, bits, space, keys = dims
    ext = rows + 2
    frames = q_ref.shape[2]
    frame_at = lax.axis_index("frame")
    space_at = lax.axis_index("space")
    partner = []
    for b in range(bits):
        step = 1 << b
        partner.append(frame_at + step * (1 - 2 * ((frame_at // step) % 2)))
    has = (space_at > 0, space_at < space - 1)
    near = (space_at - 1, space_at + 1)

    def remote(src, dst, send, recv, frame, band):
        return pltpu.make_async_remote_copy(
            src_ref=src, dst_ref=dst, send_sem=send, recv_sem=recv,
            device_id=(frame, band), device_id_type=pl.DeviceIdType.MESH,
        )

    def kv_copy(c, b):
        return remote(
            kvx.at[c, :, :, pl.ds(0, tok)], kvx.at[c, :, :, pl.ds(tok * (b + 1), tok)],
            kv_ss.at[c, b], kv_rs.at[c, b], partner[b], space_at,
        )

    def dkv_copy(c, b):
        return remote(
            dkv_out.at[c, b], dkv_in.at[c, b], dkv_ss.at[c, b], dkv_rs.at[c, b], partner[b], space_at
        )

    def halo_copy(c, s):
        return remote(
            qg.at[c, :, 0 if s == 0 else rows - 1], halo.at[c, 1 - s],
            halo_ss.at[c, s], halo_rs.at[c, 1 - s], frame_at, near[s],
        )

    def stat_copy(c, s):
        return remote(
            stat.at[c, 2 * s], stat_in.at[c, 1 - s],
            stat_ss.at[c, s], stat_rs.at[c, 1 - s], frame_at, near[s],
        )

    def rim_copy(c, s):
        return remote(
            rim_out.at[c, s], rim_in.at[c, 1 - s],
            rim_ss.at[c, s], rim_rs.at[c, 1 - s], frame_at, near[s],
        )

    def start_sides(copy, c):
        for s in range(2):
            @pl.when(has[s])
            def _():
                copy(c, s).start()

    def wait_sides(copy, c):
        for s in range(2):
            @pl.when(has[s])
            def _():
                copy(c, 1 - s).wait_recv()

    def wait_sent_sides(copy, c):
        for s in range(2):
            @pl.when(has[s])
            def _():
                copy(c, s).wait_send()

    loads = [
        pltpu.make_async_copy(source, target, load_sem.at[n])
        for n, (source, target) in enumerate(
            ((k_hbm, k_ref), (v_hbm, v_ref), (q_hbm, q_ref), (g_hbm, g_ref), (mask_hbm, mask_ref))
        )
    ]
    for load in loads:
        load.start()

    barrier = pltpu.get_barrier_semaphore()
    for b in range(bits):
        pl.semaphore_signal(
            barrier, inc=1, device_id=(partner[b], space_at), device_id_type=pl.DeviceIdType.MESH
        )
    for s in range(2):
        @pl.when(has[s])
        def _():
            pl.semaphore_signal(
                barrier, inc=1, device_id=(frame_at, near[s]), device_id_type=pl.DeviceIdType.MESH
            )
    for load in loads:
        load.wait()

    def gather(c, carry):
        at = pl.ds(pl.multiple_of(c * WIDE, WIDE), WIDE)
        for r in range(rows):
            kvx[c, 0, r, :tok] = k_ref[r, :, :, at].reshape(tok, WIDE)
            kvx[c, 1, r, :tok] = v_ref[r, :, :, at].reshape(tok, WIDE)
            query = q_ref[r, :, :, at].reshape(tok, WIDE)
            qg[c, 0, r] = (query.astype(F32) * SCALE).astype(BF16)
            qg[c, 1, r] = g_ref[r, :, :, at].reshape(tok, WIDE)
        return carry

    lax.fori_loop(0, chunks, gather, 0)

    pl.semaphore_wait(barrier, bits + has[0].astype(jnp.int32) + has[1].astype(jnp.int32))

    def send_first(c, carry):
        start_sides(halo_copy, c)
        for b in reversed(range(bits)):
            kv_copy(c, b).start()
        return carry

    lax.fori_loop(0, min(AHEAD, chunks), send_first, 0)

    low = lax.broadcasted_iota(jnp.int32, (tok, 128), 1) < HEAD_DIM

    for s in range(2):
        @pl.when(jnp.logical_not(has[s]))
        def _():
            halo[:, s] = jnp.zeros(halo.shape[:1] + halo.shape[2:], BF16)
            rim_in[:, s] = jnp.zeros(rim_in.shape[:1] + rim_in.shape[2:], BF16)
            stat_row = lax.broadcasted_iota(jnp.int32, (chunks, STATS, 128), 1)
            stat_in[:, s] = jnp.where(stat_row < HEADS, NEG, 0.0).astype(F32)

    every = mask_ref.shape[1]
    token = lax.broadcasted_iota(jnp.int32, (tok, every), 0)
    here = lax.broadcasted_iota(jnp.int32, (tok, every), 1) == frame_at * frames + token % frames
    slot = lax.broadcasted_iota(jnp.int32, (tok, keys), 1) // tok
    bias = jnp.where(slot > bits, NEG, 0.0).astype(F32)
    for b in range(bits):
        chosen = jnp.where(here, mask_ref[b : b + 1, :].astype(F32), 0.0)
        open_to = jnp.sum(chosen, axis=1, keepdims=True)
        bias = jnp.where(slot == b + 1, (1.0 - open_to) * NEG, bias)
    bias_at[...] = bias

    def stacked(block):
        wide = block.astype(F32)
        zero = jnp.zeros((tok, 128), F32)
        out = []
        for h in range(HEADS):
            half = wide[:, 128 * (h // 2) : 128 * (h // 2) + 128]
            kept = jnp.where(low if h % 2 == 0 else jnp.logical_not(low), half, zero)
            out.append(jnp.concatenate([kept, zero] if h < 2 else [zero, kept], axis=1))
        return jnp.concatenate(out, axis=0).astype(BF16)

    def picked(full):
        return jnp.concatenate(
            [
                jnp.where(low, full[:tok, :128], full[tok : 2 * tok, :128]),
                jnp.where(low, full[2 * tok : 3 * tok, 128:], full[3 * tok :, 128:]),
            ],
            axis=1,
        )

    def prepare(c, carry):
        spare = keys - tok * (bits + 1)
        if spare:
            kvx[c, :, :, keys - spare :, :] = jnp.zeros((2, rows, spare, WIDE), BF16)
        for r in range(rows):
            qm[c, r + 1] = stacked(qg[c, 0, r])
            gm[c, r + 1] = stacked(qg[c, 1, r])
        return carry

    lax.fori_loop(0, chunks, prepare, 0)

    stat_lane = lax.broadcasted_iota(jnp.int32, (tok, 128), 1)
    spare_tokens = jnp.zeros((128 - 2 * tok, 128), F32)

    def forward(c):
        bias = jnp.concatenate([bias_at[...]] * HEADS, axis=0)
        tiles = []
        for i in range(ext):
            if i == 0 or i == ext - 1:
                side = 0 if i == 0 else 1
                qm[c, i] = stacked(halo[c, side, 0])
                gm[c, i] = stacked(halo[c, side, 1])
            query, grad = qm[c, i], gm[c, i]
            near_rows = [r for r in range(rows) if 0 <= i - r <= 2]
            scores = [dot_nt(query, kvx[c, 0, r]) + bias for r in near_rows]
            top = jnp.max(functools.reduce(jnp.maximum, scores), axis=1, keepdims=True)
            probs = [jnp.exp(one - top) for one in scores]
            total = jnp.sum(functools.reduce(jnp.add, probs), axis=1, keepdims=True)
            full = None
            for r, prob in zip(near_rows, probs):
                prob = prob.astype(BF16)
                pm[c, r, i - r] = prob
                part = dot_nn(prob, kvx[c, 1, r])
                full = part if full is None else full + part
            ot[c, i] = picked(full)
            tile = jnp.zeros((tok, 128), F32)
            for h in range(HEADS):
                span = slice(h * tok, (h + 1) * tok)
                half = slice(128 * (h // 2), 128 * (h // 2) + 128)
                delta = jnp.sum(
                    full[span, half] * grad[span, half].astype(F32), axis=1, keepdims=True
                )
                for kind, value in enumerate((top[span], total[span], delta)):
                    tile = jnp.where(stat_lane == kind * HEADS + h, value, tile)
            tiles.append(tile)
        for place, at in enumerate((0, 2, ext - 2)):
            second = tiles[at + 1] if place != 1 else jnp.zeros((tok, 128), F32)
            both = jnp.concatenate([tiles[at], second, spare_tokens], axis=0)
            stat[c, place] = both.T[:STATS]

    def backward(c):
        turned = []
        for place in range(3):
            mine = stat[c, place]
            top, total, delta = (mine[k * HEADS : (k + 1) * HEADS] for k in range(3))
            if place == 1:
                alpha = 1.0 / total
                delta = delta * alpha
            else:
                theirs = stat_in[c, place // 2]
                top2, total2, delta2 = (theirs[k * HEADS : (k + 1) * HEADS] for k in range(3))
                best = jnp.maximum(top, top2)
                part, part2 = jnp.exp(top - best), jnp.exp(top2 - best)
                inverse = 1.0 / (total * part + total2 * part2)
                alpha = part * inverse
                delta = (delta * part + delta2 * part2) * inverse
            both = jnp.concatenate(
                [alpha, delta, jnp.zeros((128 - 2 * HEADS, 128), F32)], axis=0
            )
            turned.append(both.T)
        for i in range(ext):
            place = 0 if i < 2 else (1 if i < ext - 2 else 2)
            base = tok if i in (1, ext - 1) else 0
            columns = turned[place][base : base + tok]
            alpha_h = [columns[:, h : h + 1] for h in range(HEADS)]
            alpha = jnp.concatenate(alpha_h, axis=0)
            delta = jnp.concatenate([columns[:, HEADS + h : HEADS + h + 1] for h in range(HEADS)], axis=0)
            full = None
            for r in range(rows):
                if not 0 <= i - r <= 2:
                    continue
                grad_prob = dot_nt(gm[c, i], kvx[c, 1, r])
                weight = pm[c, r, i - r].astype(F32) * alpha
                grad_score = (weight * (grad_prob - delta)).astype(BF16)
                wm[r, i - r] = weight.astype(BF16)
                dm[r, i - r] = grad_score
                part = dot_nn(grad_score, kvx[c, 0, r])
                full = part if full is None else full + part
            query_grad = picked(full) * SCALE
            spread = jnp.concatenate(
                [jnp.where(low, alpha_h[0], alpha_h[1]), jnp.where(low, alpha_h[2], alpha_h[3])], axis=1
            )
            attended = ot[c, i] * spread
            if i == 0 or i == ext - 1:
                s = 0 if i == 0 else 1
                rim_out[c, s, 0] = attended.astype(BF16)
                rim_out[c, s, 1] = query_grad.astype(BF16)
            else:
                oq[c, 0, i - 1] = attended
                oq[c, 1, i - 1] = query_grad
        for r in range(rows):
            grads = gm[c, r : r + 3].reshape(3 * HEADS * tok, WIDE)
            queries = qm[c, r : r + 3].reshape(3 * HEADS * tok, WIDE)
            key_grad = dot_tn(dm[r].reshape(3 * HEADS * tok, keys), queries)
            value_grad = dot_tn(wm[r].reshape(3 * HEADS * tok, keys), grads)
            for which, result in enumerate((key_grad, value_grad)):
                dkv[c, which, r] = result[:tok]
                for b in range(bits):
                    dkv_out[c, b, which, r] = result[tok * (b + 1) : tok * (b + 2)].astype(BF16)

    def step(t, carry):
        @pl.when(t < chunks)
        def _():
            for b in range(bits):
                kv_copy(t, b).wait_recv()

            @pl.when(t + AHEAD < chunks)
            def _():
                send_first(t + AHEAD, 0)

            wait_sides(halo_copy, t)
            forward(t)
            start_sides(stat_copy, t)

        @pl.when(t > 0)
        def _():
            wait_sides(stat_copy, t - 1)
            backward(t - 1)
            for b in reversed(range(bits)):
                dkv_copy(t - 1, b).start()
            start_sides(rim_copy, t - 1)

        return carry

    lax.fori_loop(0, chunks + 1, step, 0)

    def finish(c, carry):
        at = pl.ds(pl.multiple_of(c * WIDE, WIDE), WIDE)
        shape = (tok // frames, frames, WIDE)
        wait_sides(rim_copy, c)
        for r in range(rows):
            for which in range(2):
                result = oq[c, which, r]
                if r == 0:
                    result = result + rim_in[c, 0, which].astype(F32)
                if r == rows - 1:
                    result = result + rim_in[c, 1, which].astype(F32)
                out_ref[which, r, :, :, at] = result.astype(BF16).reshape(shape)
        for b in range(bits):
            dkv_copy(c, b).wait_recv()
        for r in range(rows):
            for which in range(2):
                result = dkv[c, which, r]
                for b in range(bits):
                    result = result + dkv_in[c, b, which, r].astype(F32)
                out_ref[2 + which, r, :, :, at] = result.astype(BF16).reshape(shape)
        return carry

    lax.fori_loop(0, chunks, finish, 0)

    def drain(c, carry):
        for b in range(bits):
            kv_copy(c, b).wait_send()
            dkv_copy(c, b).wait_send()
        wait_sent_sides(halo_copy, c)
        wait_sent_sides(stat_copy, c)
        wait_sent_sides(rim_copy, c)
        return carry

    lax.fori_loop(0, chunks, drain, 0)


def settle(in_ref, *refs):
    outs, (held, in_sem, out_sem) = refs[:-3], refs[-3:]
    fetches = [
        pltpu.make_async_copy(in_ref.at[n], held.at[n], in_sem.at[n]) for n in range(len(outs))
    ]
    stores = [pltpu.make_async_copy(held.at[n], out, out_sem.at[n]) for n, out in enumerate(outs)]
    for fetch in fetches:
        fetch.start()
    for fetch, store in zip(fetches, stores):
        fetch.wait()
        store.start()
    for store in stores:
        store.wait()


def per_device(query_vectors, key_vectors, value_vectors, out_cotangent, partner_mask):
    frames, rows, cols, width = query_vectors.shape
    bits = min(4, lax.axis_size("frame").bit_length() - 1)
    space = lax.axis_size("space")
    chunks = width // WIDE
    tok = frames * cols
    keys = -(-tok * (bits + 1) // 128) * 128
    ext = rows + 2
    arrays = [
        array.transpose(1, 2, 0, 3)
        for array in (query_vectors, key_vectors, value_vectors, out_cotangent)
    ]

    dims = (chunks, rows, tok, bits, space, keys)
    vmem = pl.BlockSpec(memory_space=pltpu.VMEM)
    stack = HEADS * tok
    dma = pltpu.SemaphoreType.DMA
    result = pl.pallas_call(
        functools.partial(kernel, dims),
        out_shape=jax.ShapeDtypeStruct((4, rows, cols, frames, width), BF16),
        in_specs=[pl.BlockSpec(memory_space=pl.ANY)] * 5,
        out_specs=vmem,
        scratch_shapes=[
            *[pltpu.VMEM((rows, cols, frames, width), BF16)] * 4,
            pltpu.VMEM(partner_mask.shape[::-1], jnp.int32),
            pltpu.VMEM((chunks, 2, rows, keys, WIDE), BF16),
            pltpu.VMEM((chunks, 2, rows, tok, WIDE), BF16),
            pltpu.VMEM((chunks, 2, 2, tok, WIDE), BF16),
            pltpu.VMEM((tok, keys), F32),
            pltpu.VMEM((chunks, ext, stack, WIDE), BF16),
            pltpu.VMEM((chunks, ext, stack, WIDE), BF16),
            pltpu.VMEM((chunks, rows, 3, stack, keys), BF16),
            pltpu.VMEM((chunks, ext, tok, WIDE), F32),
            pltpu.VMEM((chunks, 3, STATS, 128), F32),
            pltpu.VMEM((chunks, 2, STATS, 128), F32),
            pltpu.VMEM((rows, 3, stack, keys), BF16),
            pltpu.VMEM((rows, 3, stack, keys), BF16),
            pltpu.VMEM((chunks, 2, rows, tok, WIDE), F32),
            pltpu.VMEM((chunks, 2, 2, tok, WIDE), BF16),
            pltpu.VMEM((chunks, 2, 2, tok, WIDE), BF16),
            pltpu.VMEM((chunks, 2, rows, tok, WIDE), F32),
            pltpu.VMEM((chunks, bits, 2, rows, tok, WIDE), BF16),
            pltpu.VMEM((chunks, bits, 2, rows, tok, WIDE), BF16),
            dma((chunks, bits)), dma((chunks, bits)),
            dma((chunks, 2)), dma((chunks, 2)),
            dma((chunks, 2)), dma((chunks, 2)),
            dma((chunks, 2)), dma((chunks, 2)),
            dma((chunks, bits)), dma((chunks, bits)),
            dma((5,)),
        ],
        compiler_params=pltpu.CompilerParams(
            collective_id=0, has_side_effects=True, vmem_limit_bytes=60 * 1024 * 1024
        ),
        name="butterfly",
    )(*arrays, partner_mask.T)
    where = pl.BlockSpec(memory_space=pl.ANY)
    outs = pl.pallas_call(
        settle,
        out_shape=(jax.ShapeDtypeStruct((rows, cols, frames, width), BF16),) * 4,
        in_specs=[where],
        out_specs=(where,) * 4,
        scratch_shapes=[pltpu.VMEM((4, rows, cols, frames, width), BF16), dma((4,)), dma((4,))],
        name="settle",
    )(result)
    return tuple(out.transpose(2, 0, 1, 3) for out in outs)


def solution(mesh):
    spread = P("frame", "space", None, None)
    return jax.shard_map(
        per_device,
        mesh=mesh,
        in_specs=(spread,) * 4 + (P(),),
        out_specs=(spread,) * 4,
        check_vma=False,
    )
```

```python
import functools

import jax
import jax.numpy as jnp
from jax import lax
from jax.experimental import pallas as pl
from jax.experimental.pallas import tpu as pltpu
from jax.sharding import PartitionSpec as P

HEAD_DIM = 64
SCALE = 0.125
NEG = -1e30
AHEAD = 2
WIDE = 256
HEADS = WIDE // HEAD_DIM
STATS = 4 * HEADS
SENT = 2 * HEADS
F32 = jnp.float32
BF16 = jnp.bfloat16


def dot_nt(a, b):
    return lax.dot_general(a, b, (((1,), (1,)), ((), ())), preferred_element_type=F32)


def dot_nn(a, b):
    return lax.dot_general(a, b, (((1,), (0,)), ((), ())), preferred_element_type=F32)


def dot_tn(a, b):
    return lax.dot_general(a, b, (((0,), (0,)), ((), ())), preferred_element_type=F32)


def kernel(
    dims, q_hbm, k_hbm, v_hbm, g_hbm, mask_hbm, out_ref,
    k_ref, v_ref, q_ref, g_ref, mask_ref, kvx, qg, halo, bias_at, qm, gm, pm, ot, stat, stat_in, wm, dm, oq, rim_out, rim_in, dkv, dkv_out, dkv_in,
    kv_ss, kv_rs, halo_ss, halo_rs, stat_ss, stat_rs, rim_ss, rim_rs, dkv_ss, dkv_rs, load_sem,
):
    chunks, rows, tok, bits, space, keys = dims
    ext = rows + 2
    frames = q_ref.shape[2]
    frame_at = lax.axis_index("frame")
    space_at = lax.axis_index("space")
    partner = []
    for b in range(bits):
        step = 1 << b
        partner.append(frame_at + step * (1 - 2 * ((frame_at // step) % 2)))
    has = (space_at > 0, space_at < space - 1)
    near = (space_at - 1, space_at + 1)

    def remote(src, dst, send, recv, frame, band):
        return pltpu.make_async_remote_copy(
            src_ref=src, dst_ref=dst, send_sem=send, recv_sem=recv,
            device_id=(frame, band), device_id_type=pl.DeviceIdType.MESH,
        )

    def kv_copy(c, b):
        return remote(
            kvx.at[c, :, :, pl.ds(0, tok)], kvx.at[c, :, :, pl.ds(tok * (b + 1), tok)],
            kv_ss.at[c, b], kv_rs.at[c, b], partner[b], space_at,
        )

    def dkv_copy(c, b):
        return remote(
            dkv_out.at[c, b], dkv_in.at[c, b], dkv_ss.at[c, b], dkv_rs.at[c, b], partner[b], space_at
        )

    def halo_copy(c, s):
        return remote(
            qg.at[c, :, 0 if s == 0 else rows - 1], halo.at[c, 1 - s],
            halo_ss.at[c, s], halo_rs.at[c, 1 - s], frame_at, near[s],
        )

    def stat_copy(c, s):
        return remote(
            stat.at[c, 2 * s, pl.ds(0, SENT)], stat_in.at[c, 1 - s],
            stat_ss.at[c, s], stat_rs.at[c, 1 - s], frame_at, near[s],
        )

    def rim_copy(c, s):
        return remote(
            rim_out.at[c, s], rim_in.at[c, 1 - s],
            rim_ss.at[c, s], rim_rs.at[c, 1 - s], frame_at, near[s],
        )

    def start_sides(copy, c):
        for s in range(2):
            @pl.when(has[s])
            def _():
                copy(c, s).start()

    def wait_sides(copy, c):
        for s in range(2):
            @pl.when(has[s])
            def _():
                copy(c, 1 - s).wait_recv()

    def wait_sent_sides(copy, c):
        for s in range(2):
            @pl.when(has[s])
            def _():
                copy(c, s).wait_send()

    loads = [
        pltpu.make_async_copy(source, target, load_sem.at[n])
        for n, (source, target) in enumerate(
            ((k_hbm, k_ref), (v_hbm, v_ref), (q_hbm, q_ref), (g_hbm, g_ref), (mask_hbm, mask_ref))
        )
    ]
    for load in loads:
        load.start()

    barrier = pltpu.get_barrier_semaphore()
    for b in range(bits):
        pl.semaphore_signal(
            barrier, inc=1, device_id=(partner[b], space_at), device_id_type=pl.DeviceIdType.MESH
        )
    for s in range(2):
        @pl.when(has[s])
        def _():
            pl.semaphore_signal(
                barrier, inc=1, device_id=(frame_at, near[s]), device_id_type=pl.DeviceIdType.MESH
            )
    for load in loads:
        load.wait()

    def gather(c, carry):
        at = pl.ds(pl.multiple_of(c * WIDE, WIDE), WIDE)
        for r in range(rows):
            kvx[c, 0, r, :tok] = k_ref[r, :, :, at].reshape(tok, WIDE)
            kvx[c, 1, r, :tok] = v_ref[r, :, :, at].reshape(tok, WIDE)
            query = q_ref[r, :, :, at].reshape(tok, WIDE)
            qg[c, 0, r] = (query.astype(F32) * SCALE).astype(BF16)
            qg[c, 1, r] = g_ref[r, :, :, at].reshape(tok, WIDE)
        return carry

    gather(0, 0)

    pl.semaphore_wait(barrier, bits + has[0].astype(jnp.int32) + has[1].astype(jnp.int32))

    def send_first(c, carry):
        start_sides(halo_copy, c)
        for b in reversed(range(bits)):
            kv_copy(c, b).start()
        return carry

    send_first(0, 0)

    def gather_on(c, carry):
        gather(c, 0)

        @pl.when(c < AHEAD)
        def _():
            send_first(c, 0)

        return carry

    lax.fori_loop(1, chunks, gather_on, 0)

    low = lax.broadcasted_iota(jnp.int32, (tok, 128), 1) < HEAD_DIM

    for s in range(2):
        @pl.when(jnp.logical_not(has[s]))
        def _():
            halo[:, s] = jnp.zeros(halo.shape[:1] + halo.shape[2:], BF16)
            rim_in[:, s] = jnp.zeros(rim_in.shape[:1] + rim_in.shape[2:], BF16)
            stat_row = lax.broadcasted_iota(jnp.int32, (chunks, SENT, 128), 1)
            stat_in[:, s] = jnp.where(stat_row < HEADS, NEG, 0.0).astype(F32)

    every = mask_ref.shape[1]
    token = lax.broadcasted_iota(jnp.int32, (tok, every), 0)
    here = lax.broadcasted_iota(jnp.int32, (tok, every), 1) == frame_at * frames + token % frames
    slot = lax.broadcasted_iota(jnp.int32, (tok, keys), 1) // tok
    bias = jnp.where(slot > bits, NEG, 0.0).astype(F32)
    for b in range(bits):
        chosen = jnp.where(here, mask_ref[b : b + 1, :].astype(F32), 0.0)
        open_to = jnp.sum(chosen, axis=1, keepdims=True)
        bias = jnp.where(slot == b + 1, (1.0 - open_to) * NEG, bias)
    bias_at[...] = bias

    def stacked(block):
        wide = block.astype(F32)
        zero = jnp.zeros((tok, 128), F32)
        out = []
        for h in range(HEADS):
            half = wide[:, 128 * (h // 2) : 128 * (h // 2) + 128]
            kept = jnp.where(low if h % 2 == 0 else jnp.logical_not(low), half, zero)
            out.append(jnp.concatenate([kept, zero] if h < 2 else [zero, kept], axis=1))
        return jnp.concatenate(out, axis=0).astype(BF16)

    def picked(full):
        return jnp.concatenate(
            [
                jnp.where(low, full[:tok, :128], full[tok : 2 * tok, :128]),
                jnp.where(low, full[2 * tok : 3 * tok, 128:], full[3 * tok :, 128:]),
            ],
            axis=1,
        )

    def prepare(c, carry):
        spare = keys - tok * (bits + 1)
        if spare:
            kvx[c, :, :, keys - spare :, :] = jnp.zeros((2, rows, spare, WIDE), BF16)
        for r in range(rows):
            qm[c, r + 1] = stacked(qg[c, 0, r])
            gm[c, r + 1] = stacked(qg[c, 1, r])
        return carry

    lax.fori_loop(0, chunks, prepare, 0)

    stat_lane = lax.broadcasted_iota(jnp.int32, (tok, 128), 1)
    spare_tokens = jnp.zeros((128 - 2 * tok, 128), F32)

    def forward(c):
        bias = jnp.concatenate([bias_at[...]] * HEADS, axis=0)
        tiles = []
        for i in range(ext):
            if i == 0 or i == ext - 1:
                side = 0 if i == 0 else 1
                qm[c, i] = stacked(halo[c, side, 0])
                gm[c, i] = stacked(halo[c, side, 1])
            query, grad = qm[c, i], gm[c, i]
            near_rows = [r for r in range(rows) if 0 <= i - r <= 2]
            scores = [dot_nt(query, kvx[c, 0, r]) + bias for r in near_rows]
            top = jnp.max(functools.reduce(jnp.maximum, scores), axis=1, keepdims=True)
            probs = [jnp.exp(one - top) for one in scores]
            total = jnp.sum(functools.reduce(jnp.add, probs), axis=1, keepdims=True)
            full = None
            for r, prob in zip(near_rows, probs):
                prob = prob.astype(BF16)
                pm[c, r, i - r] = prob
                part = dot_nn(prob, kvx[c, 1, r])
                full = part if full is None else full + part
            ot[c, i] = picked(full)
            inverse = 1.0 / total
            log_total = top + jnp.log(total)
            tile = jnp.zeros((tok, 128), F32)
            for h in range(HEADS):
                span = slice(h * tok, (h + 1) * tok)
                half = slice(128 * (h // 2), 128 * (h // 2) + 128)
                delta = inverse[span] * jnp.sum(
                    full[span, half] * grad[span, half].astype(F32), axis=1, keepdims=True
                )
                for kind, value in enumerate((log_total[span], delta, top[span])):
                    tile = jnp.where(stat_lane == kind * HEADS + h, value, tile)
            tiles.append(tile)
        for place, at in enumerate((0, 2, ext - 2)):
            second = tiles[at + 1] if place != 1 else jnp.zeros((tok, 128), F32)
            both = jnp.concatenate([tiles[at], second, spare_tokens], axis=0)
            stat[c, place] = both.T[:STATS]

    def backward(c):
        turned = []
        for place in range(3):
            mine = stat[c, place]
            log_total, delta, top = (mine[k * HEADS : (k + 1) * HEADS] for k in range(3))
            if place != 1:
                theirs = stat_in[c, place // 2]
                log_total2, delta2 = (theirs[k * HEADS : (k + 1) * HEADS] for k in range(2))
                best = jnp.maximum(log_total, log_total2)
                part, part2 = jnp.exp(log_total - best), jnp.exp(log_total2 - best)
                delta = (delta * part + delta2 * part2) / (part + part2)
                log_total = best + jnp.log(part + part2)
            alpha = jnp.exp(top - log_total)
            both = jnp.concatenate(
                [alpha, delta, jnp.zeros((128 - 2 * HEADS, 128), F32)], axis=0
            )
            turned.append(both.T)
        for i in range(ext):
            place = 0 if i < 2 else (1 if i < ext - 2 else 2)
            base = tok if i in (1, ext - 1) else 0
            columns = turned[place][base : base + tok]
            alpha_h = [columns[:, h : h + 1] for h in range(HEADS)]
            alpha = jnp.concatenate(alpha_h, axis=0)
            delta = jnp.concatenate([columns[:, HEADS + h : HEADS + h + 1] for h in range(HEADS)], axis=0)
            full = None
            for r in range(rows):
                if not 0 <= i - r <= 2:
                    continue
                grad_prob = dot_nt(gm[c, i], kvx[c, 1, r])
                weight = pm[c, r, i - r].astype(F32) * alpha
                grad_score = (weight * (grad_prob - delta)).astype(BF16)
                wm[r, i - r] = weight.astype(BF16)
                dm[r, i - r] = grad_score
                part = dot_nn(grad_score, kvx[c, 0, r])
                full = part if full is None else full + part
            query_grad = picked(full) * SCALE
            spread = jnp.concatenate(
                [jnp.where(low, alpha_h[0], alpha_h[1]), jnp.where(low, alpha_h[2], alpha_h[3])], axis=1
            )
            attended = ot[c, i] * spread
            if i == 0 or i == ext - 1:
                s = 0 if i == 0 else 1
                rim_out[c, s, 0] = attended.astype(BF16)
                rim_out[c, s, 1] = query_grad.astype(BF16)
            else:
                oq[c, 0, i - 1] = attended
                oq[c, 1, i - 1] = query_grad
        start_sides(rim_copy, c)
        for r in range(rows):
            grads = gm[c, r : r + 3].reshape(3 * HEADS * tok, WIDE)
            queries = qm[c, r : r + 3].reshape(3 * HEADS * tok, WIDE)
            key_grad = dot_tn(dm[r].reshape(3 * HEADS * tok, keys), queries)
            value_grad = dot_tn(wm[r].reshape(3 * HEADS * tok, keys), grads)
            for which, result in enumerate((key_grad, value_grad)):
                dkv[c, which, r] = result[:tok]
                for b in range(bits):
                    dkv_out[c, b, which, r] = result[tok * (b + 1) : tok * (b + 2)].astype(BF16)

    def step(t, carry):
        @pl.when(t < chunks)
        def _():
            for b in range(bits):
                kv_copy(t, b).wait_recv()

            @pl.when(t + AHEAD < chunks)
            def _():
                send_first(t + AHEAD, 0)

            wait_sides(halo_copy, t)
            forward(t)
            start_sides(stat_copy, t)

        @pl.when(t > 0)
        def _():
            wait_sides(stat_copy, t - 1)
            backward(t - 1)
            for b in reversed(range(bits)):
                dkv_copy(t - 1, b).start()

        return carry

    lax.fori_loop(0, chunks + 1, step, 0)

    def finish(c, carry):
        at = pl.ds(pl.multiple_of(c * WIDE, WIDE), WIDE)
        shape = (tok // frames, frames, WIDE)
        wait_sides(rim_copy, c)
        for r in range(rows):
            for which in range(2):
                result = oq[c, which, r]
                if r == 0:
                    result = result + rim_in[c, 0, which].astype(F32)
                if r == rows - 1:
                    result = result + rim_in[c, 1, which].astype(F32)
                out_ref[which, r, :, :, at] = result.astype(BF16).reshape(shape)
        for b in range(bits):
            dkv_copy(c, b).wait_recv()
        for r in range(rows):
            for which in range(2):
                result = dkv[c, which, r]
                for b in range(bits):
                    result = result + dkv_in[c, b, which, r].astype(F32)
                out_ref[2 + which, r, :, :, at] = result.astype(BF16).reshape(shape)
        return carry

    lax.fori_loop(0, chunks, finish, 0)

    def drain(c, carry):
        for b in range(bits):
            kv_copy(c, b).wait_send()
            dkv_copy(c, b).wait_send()
        wait_sent_sides(halo_copy, c)
        wait_sent_sides(stat_copy, c)
        wait_sent_sides(rim_copy, c)
        return carry

    lax.fori_loop(0, chunks, drain, 0)


def settle(in_ref, *refs):
    outs, (held, in_sem, out_sem) = refs[:-3], refs[-3:]
    fetches = [
        pltpu.make_async_copy(in_ref.at[n], held.at[n], in_sem.at[n]) for n in range(len(outs))
    ]
    stores = [pltpu.make_async_copy(held.at[n], out, out_sem.at[n]) for n, out in enumerate(outs)]
    for fetch in fetches:
        fetch.start()
    for fetch, store in zip(fetches, stores):
        fetch.wait()
        store.start()
    for store in stores:
        store.wait()


def per_device(query_vectors, key_vectors, value_vectors, out_cotangent, partner_mask):
    frames, rows, cols, width = query_vectors.shape
    bits = min(4, lax.axis_size("frame").bit_length() - 1)
    space = lax.axis_size("space")
    chunks = width // WIDE
    tok = frames * cols
    keys = -(-tok * (bits + 1) // 128) * 128
    ext = rows + 2
    arrays = [
        array.transpose(1, 2, 0, 3)
        for array in (query_vectors, key_vectors, value_vectors, out_cotangent)
    ]

    dims = (chunks, rows, tok, bits, space, keys)
    vmem = pl.BlockSpec(memory_space=pltpu.VMEM)
    stack = HEADS * tok
    dma = pltpu.SemaphoreType.DMA
    result = pl.pallas_call(
        functools.partial(kernel, dims),
        out_shape=jax.ShapeDtypeStruct((4, rows, cols, frames, width), BF16),
        in_specs=[pl.BlockSpec(memory_space=pl.ANY)] * 5,
        out_specs=vmem,
        scratch_shapes=[
            *[pltpu.VMEM((rows, cols, frames, width), BF16)] * 4,
            pltpu.VMEM(partner_mask.shape[::-1], jnp.int32),
            pltpu.VMEM((chunks, 2, rows, keys, WIDE), BF16),
            pltpu.VMEM((chunks, 2, rows, tok, WIDE), BF16),
            pltpu.VMEM((chunks, 2, 2, tok, WIDE), BF16),
            pltpu.VMEM((tok, keys), F32),
            pltpu.VMEM((chunks, ext, stack, WIDE), BF16),
            pltpu.VMEM((chunks, ext, stack, WIDE), BF16),
            pltpu.VMEM((chunks, rows, 3, stack, keys), BF16),
            pltpu.VMEM((chunks, ext, tok, WIDE), F32),
            pltpu.VMEM((chunks, 3, STATS, 128), F32),
            pltpu.VMEM((chunks, 2, SENT, 128), F32),
            pltpu.VMEM((rows, 3, stack, keys), BF16),
            pltpu.VMEM((rows, 3, stack, keys), BF16),
            pltpu.VMEM((chunks, 2, rows, tok, WIDE), F32),
            pltpu.VMEM((chunks, 2, 2, tok, WIDE), BF16),
            pltpu.VMEM((chunks, 2, 2, tok, WIDE), BF16),
            pltpu.VMEM((chunks, 2, rows, tok, WIDE), F32),
            pltpu.VMEM((chunks, bits, 2, rows, tok, WIDE), BF16),
            pltpu.VMEM((chunks, bits, 2, rows, tok, WIDE), BF16),
            dma((chunks, bits)), dma((chunks, bits)),
            dma((chunks, 2)), dma((chunks, 2)),
            dma((chunks, 2)), dma((chunks, 2)),
            dma((chunks, 2)), dma((chunks, 2)),
            dma((chunks, bits)), dma((chunks, bits)),
            dma((5,)),
        ],
        compiler_params=pltpu.CompilerParams(
            collective_id=0, has_side_effects=True, vmem_limit_bytes=60 * 1024 * 1024
        ),
        name="butterfly",
    )(*arrays, partner_mask.T)
    where = pl.BlockSpec(memory_space=pl.ANY)
    outs = pl.pallas_call(
        settle,
        out_shape=(jax.ShapeDtypeStruct((rows, cols, frames, width), BF16),) * 4,
        in_specs=[where],
        out_specs=(where,) * 4,
        scratch_shapes=[pltpu.VMEM((4, rows, cols, frames, width), BF16), dma((4,)), dma((4,))],
        name="settle",
    )(result)
    return tuple(out.transpose(2, 0, 1, 3) for out in outs)


def solution(mesh):
    spread = P("frame", "space", None, None)
    return jax.shard_map(
        per_device,
        mesh=mesh,
        in_specs=(spread,) * 4 + (P(),),
        out_specs=(spread,) * 4,
        check_vma=False,
    )
```

```python
import functools

import jax
import jax.numpy as jnp
from jax import lax
from jax.experimental import pallas as pl
from jax.experimental.pallas import tpu as pltpu
from jax.sharding import PartitionSpec as P

HEAD_DIM = 64
SCALE = 0.125
NEG = -1e30
AHEAD = 2
WIDE = 256
HEADS = WIDE // HEAD_DIM
STATS = 4 * HEADS
SENT = 2 * HEADS
F32 = jnp.float32
BF16 = jnp.bfloat16


def dot_nt(a, b):
    return lax.dot_general(a, b, (((1,), (1,)), ((), ())), preferred_element_type=F32)


def dot_nn(a, b):
    return lax.dot_general(a, b, (((1,), (0,)), ((), ())), preferred_element_type=F32)


def dot_tn(a, b):
    return lax.dot_general(a, b, (((0,), (0,)), ((), ())), preferred_element_type=F32)


def kernel(
    dims, q_hbm, k_hbm, v_hbm, g_hbm, mask_hbm, out_ref,
    k_ref, v_ref, q_ref, g_ref, mask_ref, kvx, qg, halo, bias_at, qm, gm, pm, ot, stat, stat_in, wm, dm, oq, rim_out, rim_in, dkv, dkv_out, dkv_in,
    kv_ss, kv_rs, halo_ss, halo_rs, stat_ss, stat_rs, rim_ss, rim_rs, dkv_ss, dkv_rs, load_sem,
):
    chunks, rows, tok, bits, space, keys = dims
    ext = rows + 2
    frames = q_ref.shape[2]
    frame_at = lax.axis_index("frame")
    space_at = lax.axis_index("space")
    partner = []
    for b in range(bits):
        step = 1 << b
        partner.append(frame_at + step * (1 - 2 * ((frame_at // step) % 2)))
    has = (space_at > 0, space_at < space - 1)
    near = (space_at - 1, space_at + 1)

    def remote(src, dst, send, recv, frame, band):
        return pltpu.make_async_remote_copy(
            src_ref=src, dst_ref=dst, send_sem=send, recv_sem=recv,
            device_id=(frame, band), device_id_type=pl.DeviceIdType.MESH,
        )

    def kv_copy(c, b):
        return remote(
            kvx.at[c, :, :, pl.ds(0, tok)], kvx.at[c, :, :, pl.ds(tok * (b + 1), tok)],
            kv_ss.at[c, b], kv_rs.at[c, b], partner[b], space_at,
        )

    def dkv_copy(c, b):
        return remote(
            dkv_out.at[c, b], dkv_in.at[c, b], dkv_ss.at[c, b], dkv_rs.at[c, b], partner[b], space_at
        )

    def halo_copy(c, s):
        return remote(
            qg.at[c, :, 0 if s == 0 else rows - 1], halo.at[c, 1 - s],
            halo_ss.at[c, s], halo_rs.at[c, 1 - s], frame_at, near[s],
        )

    def stat_copy(c, s):
        return remote(
            stat.at[c, 2 * s, pl.ds(0, SENT)], stat_in.at[c, 1 - s],
            stat_ss.at[c, s], stat_rs.at[c, 1 - s], frame_at, near[s],
        )

    def rim_copy(c, s):
        return remote(
            rim_out.at[c, s], rim_in.at[c, 1 - s],
            rim_ss.at[c, s], rim_rs.at[c, 1 - s], frame_at, near[s],
        )

    def start_sides(copy, c):
        for s in range(2):
            @pl.when(has[s])
            def _():
                copy(c, s).start()

    def wait_sides(copy, c):
        for s in range(2):
            @pl.when(has[s])
            def _():
                copy(c, 1 - s).wait_recv()

    def wait_sent_sides(copy, c):
        for s in range(2):
            @pl.when(has[s])
            def _():
                copy(c, s).wait_send()

    loads = [
        pltpu.make_async_copy(source, target, load_sem.at[n])
        for n, (source, target) in enumerate(
            ((k_hbm, k_ref), (v_hbm, v_ref), (q_hbm, q_ref), (g_hbm, g_ref), (mask_hbm, mask_ref))
        )
    ]
    for load in loads:
        load.start()

    barrier = pltpu.get_barrier_semaphore()
    for b in range(bits):
        pl.semaphore_signal(
            barrier, inc=1, device_id=(partner[b], space_at), device_id_type=pl.DeviceIdType.MESH
        )
    for s in range(2):
        @pl.when(has[s])
        def _():
            pl.semaphore_signal(
                barrier, inc=1, device_id=(frame_at, near[s]), device_id_type=pl.DeviceIdType.MESH
            )
    for load in loads:
        load.wait()

    def gather(c, carry):
        at = pl.ds(pl.multiple_of(c * WIDE, WIDE), WIDE)
        for r in range(rows):
            kvx[c, 0, r, :tok] = k_ref[r, :, :, at].reshape(tok, WIDE)
            kvx[c, 1, r, :tok] = v_ref[r, :, :, at].reshape(tok, WIDE)
            query = q_ref[r, :, :, at].reshape(tok, WIDE)
            qg[c, 0, r] = (query.astype(F32) * SCALE).astype(BF16)
            qg[c, 1, r] = g_ref[r, :, :, at].reshape(tok, WIDE)
        return carry

    gather(0, 0)

    pl.semaphore_wait(barrier, bits + has[0].astype(jnp.int32) + has[1].astype(jnp.int32))

    def send_first(c, carry):
        start_sides(halo_copy, c)
        for b in reversed(range(bits)):
            kv_copy(c, b).start()
        return carry

    send_first(0, 0)

    def gather_on(c, carry):
        gather(c, 0)

        @pl.when(c < AHEAD)
        def _():
            send_first(c, 0)

        return carry

    lax.fori_loop(1, chunks, gather_on, 0)

    low = lax.broadcasted_iota(jnp.int32, (tok, 128), 1) < HEAD_DIM

    for s in range(2):
        @pl.when(jnp.logical_not(has[s]))
        def _():
            halo[:, s] = jnp.zeros(halo.shape[:1] + halo.shape[2:], BF16)
            rim_in[:, s] = jnp.zeros(rim_in.shape[:1] + rim_in.shape[2:], BF16)
            stat_row = lax.broadcasted_iota(jnp.int32, (chunks, SENT, 128), 1)
            stat_in[:, s] = jnp.where(stat_row < HEADS, NEG, 0.0).astype(F32)

    every = mask_ref.shape[1]
    token = lax.broadcasted_iota(jnp.int32, (tok, every), 0)
    here = lax.broadcasted_iota(jnp.int32, (tok, every), 1) == frame_at * frames + token % frames
    slot = lax.broadcasted_iota(jnp.int32, (tok, keys), 1) // tok
    bias = jnp.where(slot > bits, NEG, 0.0).astype(F32)
    for b in range(bits):
        chosen = jnp.where(here, mask_ref[b : b + 1, :].astype(F32), 0.0)
        open_to = jnp.sum(chosen, axis=1, keepdims=True)
        bias = jnp.where(slot == b + 1, (1.0 - open_to) * NEG, bias)
    bias_at[...] = bias

    def stacked(block):
        wide = block.astype(F32)
        zero = jnp.zeros((tok, 128), F32)
        out = []
        for h in range(HEADS):
            half = wide[:, 128 * (h // 2) : 128 * (h // 2) + 128]
            kept = jnp.where(low if h % 2 == 0 else jnp.logical_not(low), half, zero)
            out.append(jnp.concatenate([kept, zero] if h < 2 else [zero, kept], axis=1))
        return jnp.concatenate(out, axis=0).astype(BF16)

    def picked(full):
        return jnp.concatenate(
            [
                jnp.where(low, full[:tok, :128], full[tok : 2 * tok, :128]),
                jnp.where(low, full[2 * tok : 3 * tok, 128:], full[3 * tok :, 128:]),
            ],
            axis=1,
        )

    def prepare(c, carry):
        spare = keys - tok * (bits + 1)
        if spare:
            kvx[c, :, :, keys - spare :, :] = jnp.zeros((2, rows, spare, WIDE), BF16)
        for r in range(rows):
            qm[c, r + 1] = stacked(qg[c, 0, r])
            gm[c, r + 1] = stacked(qg[c, 1, r])
        return carry

    lax.fori_loop(0, chunks, prepare, 0)

    stat_lane = lax.broadcasted_iota(jnp.int32, (tok, 128), 1)
    spare_tokens = jnp.zeros((128 - 2 * tok, 128), F32)

    def forward(c):
        bias = jnp.concatenate([bias_at[...]] * HEADS, axis=0)
        tiles = []
        for i in range(ext):
            if i == 0 or i == ext - 1:
                side = 0 if i == 0 else 1
                qm[c, i] = stacked(halo[c, side, 0])
                gm[c, i] = stacked(halo[c, side, 1])
            query, grad = qm[c, i], gm[c, i]
            near_rows = [r for r in range(rows) if 0 <= i - r <= 2]
            scores = [dot_nt(query, kvx[c, 0, r]) + bias for r in near_rows]
            top = jnp.max(functools.reduce(jnp.maximum, scores), axis=1, keepdims=True)
            probs = [jnp.exp(one - top) for one in scores]
            total = jnp.sum(functools.reduce(jnp.add, probs), axis=1, keepdims=True)
            full = None
            for r, prob in zip(near_rows, probs):
                pm[c, r, i - r] = prob
                part = dot_nn(prob.astype(BF16), kvx[c, 1, r])
                full = part if full is None else full + part
            ot[c, i] = picked(full)
            inverse = 1.0 / total
            log_total = top + jnp.log(total)
            tile = jnp.zeros((tok, 128), F32)
            for h in range(HEADS):
                span = slice(h * tok, (h + 1) * tok)
                half = slice(128 * (h // 2), 128 * (h // 2) + 128)
                delta = inverse[span] * jnp.sum(
                    full[span, half] * grad[span, half].astype(F32), axis=1, keepdims=True
                )
                for kind, value in enumerate((log_total[span], delta, top[span])):
                    tile = jnp.where(stat_lane == kind * HEADS + h, value, tile)
            tiles.append(tile)
        for place, at in enumerate((0, 2, ext - 2)):
            second = tiles[at + 1] if place != 1 else jnp.zeros((tok, 128), F32)
            both = jnp.concatenate([tiles[at], second, spare_tokens], axis=0)
            stat[c, place] = both.T[:STATS]

    def backward(c):
        turned = []
        for place in range(3):
            mine = stat[c, place]
            log_total, delta, top = (mine[k * HEADS : (k + 1) * HEADS] for k in range(3))
            if place != 1:
                theirs = stat_in[c, place // 2]
                log_total2, delta2 = (theirs[k * HEADS : (k + 1) * HEADS] for k in range(2))
                best = jnp.maximum(log_total, log_total2)
                part, part2 = jnp.exp(log_total - best), jnp.exp(log_total2 - best)
                delta = (delta * part + delta2 * part2) / (part + part2)
                log_total = best + jnp.log(part + part2)
            alpha = jnp.exp(top - log_total)
            both = jnp.concatenate(
                [alpha, delta, jnp.zeros((128 - 2 * HEADS, 128), F32)], axis=0
            )
            turned.append(both.T)
        for i in range(ext):
            place = 0 if i < 2 else (1 if i < ext - 2 else 2)
            base = tok if i in (1, ext - 1) else 0
            columns = turned[place][base : base + tok]
            alpha_h = [columns[:, h : h + 1] for h in range(HEADS)]
            alpha = jnp.concatenate(alpha_h, axis=0)
            delta = jnp.concatenate([columns[:, HEADS + h : HEADS + h + 1] for h in range(HEADS)], axis=0)
            full = None
            for r in range(rows):
                if not 0 <= i - r <= 2:
                    continue
                grad_prob = dot_nt(gm[c, i], kvx[c, 1, r])
                weight = pm[c, r, i - r] * alpha
                grad_score = (weight * (grad_prob - delta)).astype(BF16)
                wm[r, i - r] = weight.astype(BF16)
                dm[r, i - r] = grad_score
                part = dot_nn(grad_score, kvx[c, 0, r])
                full = part if full is None else full + part
            query_grad = picked(full) * SCALE
            spread = jnp.concatenate(
                [jnp.where(low, alpha_h[0], alpha_h[1]), jnp.where(low, alpha_h[2], alpha_h[3])], axis=1
            )
            attended = ot[c, i] * spread
            if i == 0 or i == ext - 1:
                s = 0 if i == 0 else 1
                rim_out[c, s, 0] = attended.astype(BF16)
                rim_out[c, s, 1] = query_grad.astype(BF16)
            else:
                oq[c, 0, i - 1] = attended
                oq[c, 1, i - 1] = query_grad
        start_sides(rim_copy, c)
        for r in range(rows):
            grads = gm[c, r : r + 3].reshape(3 * HEADS * tok, WIDE)
            queries = qm[c, r : r + 3].reshape(3 * HEADS * tok, WIDE)
            key_grad = dot_tn(dm[r].reshape(3 * HEADS * tok, keys), queries)
            value_grad = dot_tn(wm[r].reshape(3 * HEADS * tok, keys), grads)
            for which, result in enumerate((key_grad, value_grad)):
                dkv[c, which, r] = result[:tok]
                for b in range(bits):
                    dkv_out[c, b, which, r] = result[tok * (b + 1) : tok * (b + 2)].astype(BF16)

    def step(t, carry):
        @pl.when(t < chunks)
        def _():
            for b in range(bits):
                kv_copy(t, b).wait_recv()

            @pl.when(t + AHEAD < chunks)
            def _():
                send_first(t + AHEAD, 0)

            wait_sides(halo_copy, t)
            forward(t)
            start_sides(stat_copy, t)

        @pl.when(t > 0)
        def _():
            wait_sides(stat_copy, t - 1)
            backward(t - 1)
            for b in reversed(range(bits)):
                dkv_copy(t - 1, b).start()

        return carry

    lax.fori_loop(0, chunks + 1, step, 0)

    def finish(c, carry):
        at = pl.ds(pl.multiple_of(c * WIDE, WIDE), WIDE)
        shape = (tok // frames, frames, WIDE)
        wait_sides(rim_copy, c)
        for r in range(rows):
            for which in range(2):
                result = oq[c, which, r]
                if r == 0:
                    result = result + rim_in[c, 0, which].astype(F32)
                if r == rows - 1:
                    result = result + rim_in[c, 1, which].astype(F32)
                out_ref[which, r, :, :, at] = result.astype(BF16).reshape(shape)
        for b in range(bits):
            dkv_copy(c, b).wait_recv()
        for r in range(rows):
            for which in range(2):
                result = dkv[c, which, r]
                for b in range(bits):
                    result = result + dkv_in[c, b, which, r].astype(F32)
                out_ref[2 + which, r, :, :, at] = result.astype(BF16).reshape(shape)
        return carry

    lax.fori_loop(0, chunks, finish, 0)

    def drain(c, carry):
        for b in range(bits):
            kv_copy(c, b).wait_send()
            dkv_copy(c, b).wait_send()
        wait_sent_sides(halo_copy, c)
        wait_sent_sides(stat_copy, c)
        wait_sent_sides(rim_copy, c)
        return carry

    lax.fori_loop(0, chunks, drain, 0)


def settle(in_ref, *refs):
    outs, (held, in_sem, out_sem) = refs[:-3], refs[-3:]
    fetches = [
        pltpu.make_async_copy(in_ref.at[n], held.at[n], in_sem.at[n]) for n in range(len(outs))
    ]
    stores = [pltpu.make_async_copy(held.at[n], out, out_sem.at[n]) for n, out in enumerate(outs)]
    for fetch in fetches:
        fetch.start()
    for fetch, store in zip(fetches, stores):
        fetch.wait()
        store.start()
    for store in stores:
        store.wait()


def per_device(query_vectors, key_vectors, value_vectors, out_cotangent, partner_mask):
    frames, rows, cols, width = query_vectors.shape
    bits = min(4, lax.axis_size("frame").bit_length() - 1)
    space = lax.axis_size("space")
    chunks = width // WIDE
    tok = frames * cols
    keys = -(-tok * (bits + 1) // 128) * 128
    ext = rows + 2
    arrays = [
        array.transpose(1, 2, 0, 3)
        for array in (query_vectors, key_vectors, value_vectors, out_cotangent)
    ]

    dims = (chunks, rows, tok, bits, space, keys)
    vmem = pl.BlockSpec(memory_space=pltpu.VMEM)
    stack = HEADS * tok
    dma = pltpu.SemaphoreType.DMA
    result = pl.pallas_call(
        functools.partial(kernel, dims),
        out_shape=jax.ShapeDtypeStruct((4, rows, cols, frames, width), BF16),
        in_specs=[pl.BlockSpec(memory_space=pl.ANY)] * 5,
        out_specs=vmem,
        scratch_shapes=[
            *[pltpu.VMEM((rows, cols, frames, width), BF16)] * 4,
            pltpu.VMEM(partner_mask.shape[::-1], jnp.int32),
            pltpu.VMEM((chunks, 2, rows, keys, WIDE), BF16),
            pltpu.VMEM((chunks, 2, rows, tok, WIDE), BF16),
            pltpu.VMEM((chunks, 2, 2, tok, WIDE), BF16),
            pltpu.VMEM((tok, keys), F32),
            pltpu.VMEM((chunks, ext, stack, WIDE), BF16),
            pltpu.VMEM((chunks, ext, stack, WIDE), BF16),
            pltpu.VMEM((chunks, rows, 3, stack, keys), F32),
            pltpu.VMEM((chunks, ext, tok, WIDE), F32),
            pltpu.VMEM((chunks, 3, STATS, 128), F32),
            pltpu.VMEM((chunks, 2, SENT, 128), F32),
            pltpu.VMEM((rows, 3, stack, keys), BF16),
            pltpu.VMEM((rows, 3, stack, keys), BF16),
            pltpu.VMEM((chunks, 2, rows, tok, WIDE), F32),
            pltpu.VMEM((chunks, 2, 2, tok, WIDE), BF16),
            pltpu.VMEM((chunks, 2, 2, tok, WIDE), BF16),
            pltpu.VMEM((chunks, 2, rows, tok, WIDE), F32),
            pltpu.VMEM((chunks, bits, 2, rows, tok, WIDE), BF16),
            pltpu.VMEM((chunks, bits, 2, rows, tok, WIDE), BF16),
            dma((chunks, bits)), dma((chunks, bits)),
            dma((chunks, 2)), dma((chunks, 2)),
            dma((chunks, 2)), dma((chunks, 2)),
            dma((chunks, 2)), dma((chunks, 2)),
            dma((chunks, bits)), dma((chunks, bits)),
            dma((5,)),
        ],
        compiler_params=pltpu.CompilerParams(
            collective_id=0, has_side_effects=True, vmem_limit_bytes=60 * 1024 * 1024
        ),
        name="butterfly",
    )(*arrays, partner_mask.T)
    where = pl.BlockSpec(memory_space=pl.ANY)
    outs = pl.pallas_call(
        settle,
        out_shape=(jax.ShapeDtypeStruct((rows, cols, frames, width), BF16),) * 4,
        in_specs=[where],
        out_specs=(where,) * 4,
        scratch_shapes=[pltpu.VMEM((4, rows, cols, frames, width), BF16), dma((4,)), dma((4,))],
        name="settle",
    )(result)
    return tuple(out.transpose(2, 0, 1, 3) for out in outs)


def solution(mesh):
    spread = P("frame", "space", None, None)
    return jax.shard_map(
        per_device,
        mesh=mesh,
        in_specs=(spread,) * 4 + (P(),),
        out_specs=(spread,) * 4,
        check_vma=False,
    )
```
